256 devices in a mesh: seq: 32 (over y, z_lo, core), head: 8 (over x, z_hi).
Axes of the slice: x: 4, y: 4, z: 8 (z_hi: 2, z_lo: 4; z = z_hi * 4 + z_lo), core: 2. Of those that a mesh axis runs over, the one named last changes fastest.
Arguments:
- latent_queries: bfloat16 [4096, 128, 576], P('seq', 'head'), may hold values from -16 to 16
- latent_keys: bfloat16 [2048, 576], P('seq'), may hold values from -6 to 6
- index_queries: bfloat16 [4096, 64, 128], P('seq', 'head'), may hold values from -8 to 8
- index_keys: bfloat16 [2048, 128], P('seq'), may hold values from -6 to 6
- head_weights: float32 [4096, 64], P('seq', 'head'), may hold values from -18 to 18
- visible: int32 [4096], P('seq'), may hold values from 1 to 2048, as said below
Outputs:
- grad_index_queries: bfloat16 [4096, 64, 128], P('seq', 'head')
- grad_head_weights: float32 [4096, 64], P('seq', 'head')
- grad_index_keys: float32 [2048, 128], P('seq')
The draws below stay inside these ranges and needn't reach their ends.
Inputs may be any that keep to these rules, and one draw needn't show every extreme that they name: Row t sees keys 0 to visible[t] - 1, never more than (t * 2048) // 4096 + 1 of them; the last row sees all 2048 keys.
All inputs are finite; a program needn't handle non-finite values.
Results may differ from the reference program's by a relative error of at most 0.0049.
Values may be sent and summed in bfloat16 or wider, within the bound.
No kernel may reach another device: no remote copies, remote signals or barrier semaphores. Data moves between devices by JAX's collectives and lax.ppermute only.
A program may use at most 64 MiB of HBM per device.

```python
import math
import jax
import jax.numpy as jnp
from jax import lax

LATENT = 576
MLA_HEADS = 128
INDEX_HEADS = 64
INDEX_DIM = 128
QUERIES = 4096
KEYS = 2048


def visible_counts(key):
    positions = jnp.arange(QUERIES, dtype=jnp.int32)
    baseline = positions * KEYS // QUERIES + 1
    jitter = jax.random.randint(jax.random.fold_in(key, 11), (QUERIES,), 0, KEYS // 8 + 1)
    jitter = jnp.where(positions == QUERIES - 1, 0, jitter)
    lowest = jnp.minimum(baseline, 2)
    return jnp.maximum(baseline - jitter, lowest).astype(jnp.int32)


def make_keys(key, salt, width):
    subkey = jax.random.fold_in(key, salt)
    return jnp.clip(jax.random.normal(subkey, (KEYS, width), jnp.float32), -6.0, 6.0)


def draw_visible(key, part):
    return visible_counts(key)


def draw_latent_keys(key, part):
    return make_keys(key, 1, LATENT).astype(jnp.bfloat16)


def draw_index_keys(key, part):
    return make_keys(key, 2, INDEX_DIM).astype(jnp.bfloat16)


def draw_latent_queries(key, part):
    full_shape = (QUERIES, MLA_HEADS, LATENT)
    subkey = jax.random.fold_in(key, 3)
    values = jnp.clip(jax.random.normal(subkey, full_shape, jnp.float32), -6.0, 6.0) * 2.3
    return values.astype(jnp.bfloat16)


def draw_index_queries(key, part):
    full_shape = (QUERIES, INDEX_HEADS, INDEX_DIM)
    subkey = jax.random.fold_in(key, 5)
    values = jnp.clip(jax.random.normal(subkey, full_shape, jnp.float32), -6.0, 6.0)
    return values.astype(jnp.bfloat16)


def draw_head_weights(key, part):
    subkey = jax.random.fold_in(key, 6)
    values = jnp.clip(jax.random.normal(subkey, (QUERIES, INDEX_HEADS), jnp.float32), -6.0, 6.0) * 3.0
    return values.astype(jnp.float32)


def setup_inputs(seed: int = 0) -> dict:
    streams_of = jax.random.split(jax.random.key(seed), 7)
    return {
        "latent_queries": draw_latent_queries(jax.random.fold_in(streams_of[6], 71), 0),
        "latent_keys": draw_latent_keys(jax.random.fold_in(streams_of[6], 71), 0),
        "index_queries": draw_index_queries(jax.random.fold_in(streams_of[6], 71), 0),
        "index_keys": draw_index_keys(jax.random.fold_in(streams_of[6], 71), 0),
        "head_weights": draw_head_weights(jax.random.fold_in(streams_of[6], 71), 0),
        "visible": draw_visible(jax.random.fold_in(streams_of[6], 71), 0),
    }


mla_scale = 192.0 ** -0.5
loss_weight = 16.0
neg_fill = -1.0e30


def reference(latent_queries, latent_keys, index_queries, index_keys, head_weights, visible):
    query_count = latent_queries.shape[0]
    key_count = latent_keys.shape[0]
    row_block = math.gcd(query_count, 128)
    block_count = query_count // row_block
    latent_wide = latent_keys.astype(jnp.float32)
    index_wide = index_keys.astype(jnp.float32)
    dot_scale = INDEX_DIM ** -0.5
    head_scale = INDEX_HEADS ** -0.5
    columns = jnp.arange(key_count, dtype=jnp.int32)

    def one_block(key_grad, inputs):
        lat_rows, idx_rows, weight_rows, seen_rows = inputs
        seen = columns[None, :] < seen_rows[:, None]
        scores = jnp.einsum("thl,kl->thk", lat_rows.astype(jnp.float32), latent_wide, precision=lax.Precision.HIGHEST) * mla_scale
        scores = jnp.where(seen[:, None, :], scores, neg_fill)
        maxima = jnp.max(scores, axis=2, keepdims=True)
        mla_norm = maxima + jnp.log(jnp.sum(jnp.exp(scores - maxima), axis=2, keepdims=True))
        target = jnp.sum(jnp.exp(scores - mla_norm), axis=1) / MLA_HEADS
        products = jnp.einsum("thd,kd->thk", idx_rows.astype(jnp.float32), index_wide, precision=lax.Precision.HIGHEST) * dot_scale
        active = jnp.maximum(products, 0.0)
        logits = jnp.sum(weight_rows[:, :, None] * active, axis=1) * head_scale
        logits = jnp.where(seen, logits, neg_fill)
        row_peak = jnp.max(logits, axis=1, keepdims=True)
        weights = jnp.exp(logits - row_peak)
        index_prob = weights / jnp.sum(weights, axis=1, keepdims=True)
        slope = loss_weight * (index_prob - target)
        edge_grad = jnp.where(products > 0.0, slope[:, None, :] * (weight_rows * head_scale)[:, :, None], 0.0).astype(jnp.bfloat16)
        edge_wide = edge_grad.astype(jnp.float32)
        query_grad = (jnp.einsum("thk,kd->thd", edge_wide, index_wide, precision=lax.Precision.HIGHEST) * dot_scale).astype(jnp.bfloat16)
        weight_grad = jnp.sum(slope[:, None, :] * active, axis=2) * head_scale
        key_term = jnp.einsum("thk,thd->kd", edge_wide, idx_rows.astype(jnp.float32), precision=lax.Precision.HIGHEST) * dot_scale
        return key_grad + key_term, (query_grad, weight_grad)

    inputs = (
        latent_queries.reshape(block_count, row_block, MLA_HEADS, LATENT),
        index_queries.reshape(block_count, row_block, INDEX_HEADS, INDEX_DIM),
        head_weights.reshape(block_count, row_block, INDEX_HEADS),
        visible.reshape(block_count, row_block),
    )
    key_grad, stacked = lax.scan(one_block, jnp.zeros((key_count, INDEX_DIM), jnp.float32), inputs)
    grad_index_queries = stacked[0].reshape(query_count, INDEX_HEADS, INDEX_DIM)
    grad_head_weights = stacked[1].reshape(query_count, INDEX_HEADS)
    return (grad_index_queries, grad_head_weights, key_grad)
```

```python
import functools

import jax
import jax.numpy as jnp
from jax import lax
from jax.experimental import pallas as pl
from jax.experimental.pallas import tpu as pltpu
from jax.sharding import Mesh, PartitionSpec as P

MLA_HEADS = 128
INDEX_HEADS = 64
LOG2E = 1.4426950408889634
mla_scale = 192.0 ** (-0.5)
loss_weight = 16.0
neg_fill = -1e30

SEQ = ("y", "z", "c")
HEAD = ("x", "w")
f32 = jnp.float32
bf16 = jnp.bfloat16
HELD = pl.BlockSpec(memory_space=pltpu.VMEM)
ANYWHERE = pl.BlockSpec(memory_space=pl.ANY)
SCALARS = pl.BlockSpec(memory_space=pltpu.SMEM)


def target_kernel(skip, base_ref, q_ref, vis_ref, *refs):
    blocks = refs[:-8]
    out_ref, index_ref, bias_ref, s_ref, p_ref, sum_ref, turn_ref, out_sem = refs[-8:]
    heads, depth, rows = q_ref.shape
    key_count = bias_ref.shape[0]
    unit = key_count // base_ref.shape[0]
    span = key_count // len(blocks)
    pairs = heads // 2
    factor = mla_scale * LOG2E

    seen = vis_ref[...]
    for i in range(key_count // unit):
        ids = lax.broadcasted_iota(jnp.int32, (unit, rows), 0) + base_ref[i]
        bias_ref[i * unit : (i + 1) * unit] = jnp.where(ids < seen, 0.0, neg_fill)

    tops, shares = {}, {}
    for step in range(pairs + 2):
        top, total = None, None
        for start in range(0, key_count, span):
            part = slice(start, start + span)
            if step < pairs:
                block = blocks[start // span]
                if step == 0:
                    index_ref[part] = block[:, :skip]
                q = jnp.concatenate([q_ref[2 * step], q_ref[2 * step + 1]], axis=1)
                bias = bias_ref[part]
                s = jnp.dot(block[:, skip : skip + depth], q, preferred_element_type=f32)
                s = s + jnp.concatenate([bias, bias], axis=1)
                s_ref[step % 2, part] = s
                high = jnp.max(s, axis=0, keepdims=True)
                top = high if top is None else jnp.maximum(top, high)
            if 0 <= step - 1 < pairs:
                p = jnp.exp2(s_ref[(step - 1) % 2, part] * factor - tops[step - 1])
                p_ref[(step - 1) % 2, part] = p
                add = jnp.sum(p, axis=0, keepdims=True)
                total = add if total is None else total + add
            if 0 <= step - 2:
                p = p_ref[step % 2, part] * shares[step - 2]
                p = p[:, :rows] + p[:, rows:]
                if step == 2:
                    sum_ref[part] = p
                else:
                    sum_ref[part] += p
        if top is not None:
            tops[step] = top * factor
        if total is not None:
            shares[step - 1] = 1.0 / (total * MLA_HEADS)
    stores = []
    for i in range(key_count // span):
        for start in range(i * span, (i + 1) * span, rows):
            turn_ref[:, start : start + rows] = sum_ref[start : start + rows].T.astype(bf16)
        part = pl.ds(i * span, span)
        stores.append(pltpu.make_async_copy(turn_ref.at[:, part], out_ref.at[:, part], out_sem.at[i]))
        stores[-1].start()
    for store in stores:
        store.wait()


def head_target(queries, blocks, visible, base, skip):
    row_count, heads, depth = queries.shape
    key_count = sum(block.shape[0] for block in blocks)
    turned = queries.transpose(1, 2, 0)
    visible = visible.reshape(1, row_count)
    outs = (
        jax.ShapeDtypeStruct((row_count, key_count), bf16),
        jax.ShapeDtypeStruct((key_count, skip), bf16),
    )
    return pl.pallas_call(
        functools.partial(target_kernel, skip),
        in_specs=[SCALARS] + [HELD] * (2 + len(blocks)),
        out_specs=[ANYWHERE, HELD],
        out_shape=outs,
        scratch_shapes=[
            pltpu.VMEM((key_count, row_count), f32),
            pltpu.VMEM((2, key_count, 2 * row_count), f32),
            pltpu.VMEM((2, key_count, 2 * row_count), f32),
            pltpu.VMEM((key_count, row_count), f32),
            pltpu.VMEM((row_count, key_count), bf16),
            pltpu.SemaphoreType.DMA((len(blocks),)),
        ],
        compiler_params=pltpu.CompilerParams(vmem_limit_bytes=20 << 20),
        name="head_target",
    )(base, turned, visible, *blocks)


def pack_kernel(iq_ref, w_ref, out_ref):
    groups, count, depth = iq_ref.shape
    line = lax.broadcasted_iota(jnp.int32, (16, depth), 0)
    for g in range(groups):
        out_ref[g, :count] = iq_ref[g]
        w = w_ref[g : g + 1]
        high = w.astype(bf16).astype(f32)
        mid = (w - high).astype(bf16).astype(f32)
        low = w - high - mid
        lines = jnp.where(line == 0, high, jnp.where(line == 1, mid, jnp.where(line == 2, low, 0.0)))
        out_ref[g, count:] = lines.astype(bf16)


def pack_index(iq, weights):
    groups, count, depth = iq.shape
    return pl.pallas_call(
        pack_kernel,
        in_specs=[HELD] * 2,
        out_specs=HELD,
        out_shape=jax.ShapeDtypeStruct((groups, count + 16, depth), bf16),
        name="pack_index",
    )(iq, weights)


def unpack(got_ref, q_ref, w_ref):
    groups, lines, depth = got_ref.shape
    count = lines - 16
    for g in range(groups):
        piece = slice(g * count, (g + 1) * count)
        q_ref[piece] = got_ref[g, :count]
        w = jnp.sum(got_ref[g, count:].astype(f32), axis=0, keepdims=True)
        w = w * (INDEX_HEADS * depth) ** (-0.5)
        w_ref[piece] = jnp.broadcast_to(w, (depth, count)).T


def prob_kernel(shape, got_ref, k_ref, vis_ref, kid_ref, out_ref, q_ref, w_ref):
    groups, rows, heads = shape
    span = 512
    unpack(got_ref, q_ref, w_ref)
    w = w_ref[:, :1]
    for start in range(0, k_ref.shape[0], span):
        prod = lax.dot_general(
            q_ref[...], k_ref[start : start + span], (((1,), (1,)), ((), ())), preferred_element_type=f32
        )
        part = jnp.maximum(prod, 0.0) * w
        part = part.reshape(groups, rows, heads, span)
        part = jnp.sum(jnp.sum(part, axis=0), axis=1)
        out_ref[:, start : start + span] = part
    logits = jnp.where(kid_ref[...] < vis_ref[...], out_ref[...], neg_fill)
    peak = jnp.max(logits, axis=1, keepdims=True)
    e = jnp.exp2((logits - peak) * LOG2E)
    out_ref[...] = e * (1.0 / jnp.sum(e, axis=1, keepdims=True))


def index_prob(got, keys, visible, key_ids, shape):
    groups, rows, heads = shape
    key_count, depth = keys.shape
    count = groups * rows * heads
    return pl.pallas_call(
        functools.partial(prob_kernel, shape),
        in_specs=[HELD] * 4,
        out_specs=HELD,
        out_shape=jax.ShapeDtypeStruct((rows, key_count), f32),
        scratch_shapes=[pltpu.VMEM((count, depth), bf16), pltpu.VMEM((count, depth), f32)],
        compiler_params=pltpu.CompilerParams(vmem_limit_bytes=20 << 20),
        name="index_prob",
    )(got, keys, visible, key_ids)


def edges(shape, q, k, prob_ref, part_ref, start):
    groups, rows, heads = shape
    span = k.shape[0]
    prod = lax.dot_general(q, k, (((1,), (1,)), ((), ())), preferred_element_type=f32)
    target = jnp.sum(part_ref[:, :, start : start + span].astype(f32), axis=0)
    grad = loss_weight * (prob_ref[:, start : start + span] - target)
    wide = jnp.broadcast_to(grad[None, :, None, :], (groups, rows, heads, span))
    return jnp.where(prod > 0.0, wide.reshape(q.shape[0], span), 0.0).astype(bf16)


def key_kernel(shape, unit, slot_ref, got_ref, k_ref, prob_ref, part_ref, kg_ref, q_ref, w_ref):
    span = 512
    unpack(got_ref, q_ref, w_ref)
    q = q_ref[...]
    lift = (q.astype(f32) * w_ref[...]).T.astype(bf16)
    for start in range(0, k_ref.shape[0], span):
        edge = edges(shape, q, k_ref[start : start + span], prob_ref, part_ref, start)
        turned = jnp.dot(lift, edge, preferred_element_type=f32).T
        for i in range(span // unit):
            kg_ref[slot_ref[start // unit + i]] = turned[i * unit : (i + 1) * unit]


def query_kernel(shape, got_ref, k_ref, prob_ref, part_ref, dq_ref, acc_ref, q_ref, w_ref):
    groups, rows, heads = shape
    depth = k_ref.shape[1]
    span = 512
    unpack(got_ref, q_ref, w_ref)
    q = q_ref[...]
    for start in range(0, k_ref.shape[0], span):
        k = k_ref[start : start + span]
        edge = edges(shape, q, k, prob_ref, part_ref, start)
        step = jnp.dot(edge, k, preferred_element_type=f32)
        if start == 0:
            acc_ref[...] = step
        else:
            acc_ref[...] += step
    acc = acc_ref[...]
    group_rows = rows * heads
    scale = (INDEX_HEADS * depth) ** (-0.5)
    dq = (acc * w_ref[...]).astype(bf16)
    own = acc * q.astype(f32)
    line = lax.broadcasted_iota(jnp.int32, (16, group_rows), 0)
    for g in range(groups):
        piece = slice(g * group_rows, (g + 1) * group_rows)
        dq_ref[g, :group_rows] = dq[piece]
        dw = jnp.sum(own[piece].T, axis=0, keepdims=True) * scale
        high = dw.astype(bf16).astype(f32)
        mid = (dw - high).astype(bf16).astype(f32)
        low = dw - high - mid
        dq_ref[g, group_rows:] = jnp.where(
            line == 0, high, jnp.where(line == 1, mid, jnp.where(line == 2, low, 0.0))
        ).astype(bf16)


def key_backward(slots, got, keys, prob, parts, shape, unit):
    groups, rows, heads = shape
    key_count, depth = keys.shape
    count = groups * rows * heads
    return pl.pallas_call(
        functools.partial(key_kernel, shape, unit),
        in_specs=[SCALARS] + [HELD] * 4,
        out_specs=HELD,
        out_shape=jax.ShapeDtypeStruct((key_count // unit, unit, depth), f32),
        scratch_shapes=[pltpu.VMEM((count, depth), bf16), pltpu.VMEM((count, depth), f32)],
        compiler_params=pltpu.CompilerParams(vmem_limit_bytes=20 << 20),
        name="key_backward",
    )(slots, got, keys, prob, parts)


def query_backward(got, keys, prob, parts, shape):
    groups, rows, heads = shape
    depth = keys.shape[1]
    count = groups * rows * heads
    return pl.pallas_call(
        functools.partial(query_kernel, shape),
        in_specs=[HELD] * 4,
        out_specs=HELD,
        out_shape=jax.ShapeDtypeStruct((groups, rows * heads + 16, depth), bf16),
        scratch_shapes=[
            pltpu.VMEM((count, depth), f32),
            pltpu.VMEM((count, depth), bf16),
            pltpu.VMEM((count, depth), f32),
        ],
        compiler_params=pltpu.CompilerParams(vmem_limit_bytes=20 << 20),
        name="query_backward",
    )(got, keys, prob, parts)


def take(a, axis, shift):
    n = lax.axis_size(axis)
    return lax.ppermute(a, axis, [((i + shift) % n, i) for i in range(n)])


def take_z(a, shift):
    place = lambda i: i % 4 * 2 + i % 8 // 4
    return lax.ppermute(a, ("z", "w"), [(place(i + shift), place(i)) for i in range(8)])


def gather_keys(shard, sent):
    found = (take_z(shard, 1), take_z(shard, -1), take_z(shard, 2), sent)
    z1, z3, z2, sent = lax.optimization_barrier(found)
    row = jnp.concatenate([shard, z1, z2, z3], axis=0)
    row, sent = lax.optimization_barrier((row, sent))
    blocks = [row, take(row, "y", 1), take(row, "y", -1), take(row, "y", 2)]
    blocks += [take(block, "c", 1) for block in blocks]
    return blocks, [(dy, dz) for dy in (0, 1, 3, 2) for dz in range(4)], sent


def add_up(own, moved):
    moved = lax.optimization_barrier(moved)
    return own.astype(f32) + moved[0].astype(f32) + moved[1].astype(f32) + moved[2].astype(f32)


def pair_sum(kg, unit):
    own = kg.shape[0] // 2
    kg = kg[:own] + take(kg[own:], "c", 1)
    return kg.astype(bf16).reshape(4, 4, unit, kg.shape[-1])


def ring_sum(kg):
    kg = add_up(kg[0], (take(kg[1], "y", -1), take(kg[3], "y", 1), take(kg[2], "y", 2)))
    kg = kg.astype(bf16)
    return add_up(kg[0], (take_z(kg[1], -1), take_z(kg[3], 1), take_z(kg[2], 2)))


def body(latent_queries, latent_keys, index_queries, index_keys, head_weights, visible):
    row_count = latent_queries.shape[0]
    unit = latent_keys.shape[0]
    depth = index_keys.shape[1]
    index_heads = index_queries.shape[1]
    groups = lax.axis_size(HEAD)
    rows = row_count // groups
    me = lax.axis_index(HEAD)
    core = lax.axis_index("c")

    count = rows * index_heads
    sent = pack_index(index_queries.reshape(groups, count, depth), head_weights.reshape(groups, count))
    fill = jnp.zeros((unit, -(depth + latent_keys.shape[1]) % 128), bf16)
    blocks, places, sent = gather_keys(jnp.concatenate([index_keys, latent_keys, fill], axis=1), sent)
    chips = len(places)
    key_count = 2 * chips * unit
    dy, dz = (jnp.array([p[i] for p in places], jnp.int32) for i in range(2))
    chip = (lax.axis_index("y") + dy) % 4 * 4 + (lax.axis_index("z") + dz) % 4
    slots = jnp.concatenate([dy * 4 + dz, chips + dy * 4 + dz])
    base = jnp.concatenate([chip * 2 + core, chip * 2 + 1 - core]) * unit
    key_ids = (base[:, None] + jnp.arange(unit, dtype=jnp.int32)[None]).reshape(1, key_count)
    got = lax.all_to_all(sent, HEAD, split_axis=0, concat_axis=0, tiled=True)
    my_visible = lax.dynamic_slice_in_dim(visible, me * rows, rows, 0).reshape(rows, 1)
    shape = (groups, rows, index_heads)

    part, keys = head_target(latent_queries, blocks, visible, base, depth)
    parts = lax.all_to_all(
        part.reshape(groups, rows, key_count), HEAD, split_axis=0, concat_axis=0, tiled=True
    )
    prob = index_prob(got, keys, my_visible, key_ids, shape)
    kg = pair_sum(key_backward(slots, got, keys, prob, parts, shape, unit), unit)
    kg, prob = lax.optimization_barrier((kg, prob))
    dq = query_backward(got, keys, prob, parts, shape)
    kg = ring_sum(kg)
    high = kg.astype(bf16)
    low = (kg - high.astype(f32)).astype(bf16)
    kg = jnp.broadcast_to(jnp.concatenate([high, low], axis=0)[None], (groups, 2 * unit, depth))
    back = jnp.concatenate([dq, kg], axis=1)
    back = lax.all_to_all(back, HEAD, split_axis=0, concat_axis=0, tiled=True)
    query_grad = back[:, :count].reshape(row_count, index_heads, depth)
    weight_grad = jnp.sum(back[:, count : count + 16].astype(f32), axis=1)
    copies = back[:, count + 16 :].astype(f32)
    key_grad = jnp.sum(copies[:, :unit] + copies[:, unit:], axis=0)
    return query_grad, weight_grad.reshape(row_count, index_heads), key_grad


def solution(mesh):
    fine = Mesh(mesh.devices.reshape(4, 4, 2, 4, 2), ("y", "z", "c", "x", "w"))
    placed = (
        P(SEQ, HEAD, None),
        P(SEQ, None),
        P(SEQ, HEAD, None),
        P(SEQ, None),
        P(SEQ, HEAD),
        P(SEQ),
    )
    return jax.shard_map(
        body,
        mesh=fine,
        in_specs=placed,
        out_specs=(P(SEQ, HEAD, None), P(SEQ, HEAD), P(SEQ, None)),
        check_vma=False,
    )
```

```python
import functools

import jax
import jax.numpy as jnp
from jax import lax
from jax.experimental import pallas as pl
from jax.experimental.pallas import tpu as pltpu
from jax.sharding import Mesh, PartitionSpec as P

MLA_HEADS = 128
INDEX_HEADS = 64
LOG2E = 1.4426950408889634
mla_scale = 192.0 ** (-0.5)
loss_weight = 16.0
neg_fill = -1e30

SEQ = ("y", "z", "c")
HEAD = ("x", "w")
f32 = jnp.float32
bf16 = jnp.bfloat16
HELD = pl.BlockSpec(memory_space=pltpu.VMEM)
ANYWHERE = pl.BlockSpec(memory_space=pl.ANY)
SCALARS = pl.BlockSpec(memory_space=pltpu.SMEM)


def target_kernel(skip, base_ref, offset_ref, q_ref, vis_ref, *refs):
    index_ref, bias_ref, s_ref, p_ref, sum_ref, turn_ref, out_sem = refs[-7:]
    blocks, outs = refs[:-11], refs[-11:-7]
    heads, depth, rows = q_ref.shape
    key_count = bias_ref.shape[0]
    unit = key_count // base_ref.shape[0]
    span = key_count // len(blocks)
    pairs = heads // 2
    factor = mla_scale * LOG2E

    seen = vis_ref[...]
    for i in range(key_count // unit):
        ids = lax.broadcasted_iota(jnp.int32, (unit, rows), 0) + base_ref[i]
        bias_ref[i * unit : (i + 1) * unit] = jnp.where(ids < seen, 0.0, neg_fill)

    tops, shares = {}, {}
    for step in range(pairs + 2):
        top, total = None, None
        for start in range(0, key_count, span):
            part = slice(start, start + span)
            if step < pairs:
                block = blocks[start // span]
                if step == 0:
                    index_ref[part] = block[:, :skip]
                q = jnp.concatenate([q_ref[2 * step], q_ref[2 * step + 1]], axis=1)
                bias = bias_ref[part]
                s = jnp.dot(block[:, skip : skip + depth], q, preferred_element_type=f32)
                s = s + jnp.concatenate([bias, bias], axis=1)
                s_ref[step % 2, part] = s
                high = jnp.max(s, axis=0, keepdims=True)
                top = high if top is None else jnp.maximum(top, high)
            if 0 <= step - 1 < pairs:
                p = jnp.exp2(s_ref[(step - 1) % 2, part] * factor - tops[step - 1])
                p_ref[(step - 1) % 2, part] = p
                add = jnp.sum(p, axis=0, keepdims=True)
                total = add if total is None else total + add
            if 0 <= step - 2:
                p = p_ref[step % 2, part] * shares[step - 2]
                p = p[:, :rows] + p[:, rows:]
                if step == 2:
                    sum_ref[part] = p
                else:
                    sum_ref[part] += p
        if top is not None:
            tops[step] = top * factor
        if total is not None:
            shares[step - 1] = 1.0 / (total * MLA_HEADS)
    for start in range(0, key_count, rows):
        turn_ref[:, start : start + rows] = sum_ref[start : start + rows].T.astype(bf16)
    stores = []
    for i, out in enumerate(outs):
        for j in range(out.shape[0]):
            number = i * out.shape[0] + j
            start = pl.multiple_of(offset_ref[number], out.shape[1])
            source = turn_ref.at[pl.ds(start, out.shape[1])]
            stores.append(pltpu.make_async_copy(source, out.at[j], out_sem.at[number]))
            stores[-1].start()
    for store in stores:
        store.wait()


def head_target(queries, blocks, visible, base, offsets, skip):
    row_count, heads, depth = queries.shape
    key_count = sum(block.shape[0] for block in blocks)
    turned = queries.transpose(1, 2, 0)
    visible = visible.reshape(1, row_count)
    rows = row_count // offsets.shape[0]
    outs = [jax.ShapeDtypeStruct((offsets.shape[0] // 4, rows, key_count), bf16)] * 4
    return pl.pallas_call(
        functools.partial(target_kernel, skip),
        in_specs=[SCALARS, SCALARS] + [HELD] * (2 + len(blocks)),
        out_specs=[ANYWHERE] * 4 + [HELD],
        out_shape=outs + [jax.ShapeDtypeStruct((key_count, skip), bf16)],
        scratch_shapes=[
            pltpu.VMEM((key_count, row_count), f32),
            pltpu.VMEM((2, key_count, 2 * row_count), f32),
            pltpu.VMEM((2, key_count, 2 * row_count), f32),
            pltpu.VMEM((key_count, row_count), f32),
            pltpu.VMEM((row_count, key_count), bf16),
            pltpu.SemaphoreType.DMA((offsets.shape[0],)),
        ],
        compiler_params=pltpu.CompilerParams(vmem_limit_bytes=24 << 20),
        name="head_target",
    )(base, offsets, turned, visible, *blocks)


def pack_kernel(iq_ref, w_ref, out_ref):
    groups, count, depth = iq_ref.shape
    line = lax.broadcasted_iota(jnp.int32, (16, depth), 0)
    for g in range(groups):
        out_ref[g, :count] = iq_ref[g]
        w = w_ref[g : g + 1]
        high = w.astype(bf16).astype(f32)
        mid = (w - high).astype(bf16).astype(f32)
        low = w - high - mid
        lines = jnp.where(line == 0, high, jnp.where(line == 1, mid, jnp.where(line == 2, low, 0.0)))
        out_ref[g, count:] = lines.astype(bf16)


def pack_index(iq, weights):
    groups, count, depth = iq.shape
    return pl.pallas_call(
        pack_kernel,
        in_specs=[HELD] * 2,
        out_specs=HELD,
        out_shape=jax.ShapeDtypeStruct((groups, count + 16, depth), bf16),
        name="pack_index",
    )(iq, weights)


def unpack(got_ref, q_ref, w_ref):
    groups, lines, depth = got_ref.shape
    count = lines - 16
    for g in range(groups):
        piece = slice(g * count, (g + 1) * count)
        q_ref[piece] = got_ref[g, :count]
        w = jnp.sum(got_ref[g, count:].astype(f32), axis=0, keepdims=True)
        w = w * (INDEX_HEADS * depth) ** (-0.5)
        w_ref[piece] = jnp.broadcast_to(w, (depth, count)).T


def prob_kernel(shape, got_ref, k_ref, vis_ref, kid_ref, out_ref, q_ref, w_ref):
    groups, rows, heads = shape
    span = 512
    unpack(got_ref, q_ref, w_ref)
    w = w_ref[:, :1]
    for start in range(0, k_ref.shape[0], span):
        prod = lax.dot_general(
            q_ref[...], k_ref[start : start + span], (((1,), (1,)), ((), ())), preferred_element_type=f32
        )
        part = jnp.maximum(prod, 0.0) * w
        part = part.reshape(groups, rows, heads, span)
        part = jnp.sum(jnp.sum(part, axis=0), axis=1)
        out_ref[:, start : start + span] = part
    logits = jnp.where(kid_ref[...] < vis_ref[...], out_ref[...], neg_fill)
    peak = jnp.max(logits, axis=1, keepdims=True)
    e = jnp.exp2((logits - peak) * LOG2E)
    out_ref[...] = e * (1.0 / jnp.sum(e, axis=1, keepdims=True))


def index_prob(got, keys, visible, key_ids, shape):
    groups, rows, heads = shape
    key_count, depth = keys.shape
    count = groups * rows * heads
    return pl.pallas_call(
        functools.partial(prob_kernel, shape),
        in_specs=[HELD] * 4,
        out_specs=HELD,
        out_shape=jax.ShapeDtypeStruct((rows, key_count), f32),
        scratch_shapes=[pltpu.VMEM((count, depth), bf16), pltpu.VMEM((count, depth), f32)],
        compiler_params=pltpu.CompilerParams(vmem_limit_bytes=20 << 20),
        name="index_prob",
    )(got, keys, visible, key_ids)


def edges(shape, q, k, prob_ref, near_ref, part_ref, start):
    groups, rows, heads = shape
    span = k.shape[0]
    prod = lax.dot_general(q, k, (((1,), (1,)), ((), ())), preferred_element_type=f32)
    here = slice(start, start + span)
    target = near_ref[:, here] + part_ref[:, here].astype(f32)
    grad = loss_weight * (prob_ref[:, start : start + span] - target)
    wide = jnp.broadcast_to(grad[None, :, None, :], (groups, rows, heads, span))
    return jnp.where(prod > 0.0, wide.reshape(q.shape[0], span), 0.0).astype(bf16)


def key_kernel(shape, unit, slot_ref, got_ref, k_ref, prob_ref, near_ref, part_ref, kg_ref, q_ref, w_ref):
    span = 512
    unpack(got_ref, q_ref, w_ref)
    q = q_ref[...]
    lift = (q.astype(f32) * w_ref[...]).T.astype(bf16)
    for start in range(0, k_ref.shape[0], span):
        edge = edges(shape, q, k_ref[start : start + span], prob_ref, near_ref, part_ref, start)
        turned = jnp.dot(lift, edge, preferred_element_type=f32).T
        for i in range(span // unit):
            kg_ref[slot_ref[start // unit + i]] = turned[i * unit : (i + 1) * unit]


def query_kernel(shape, got_ref, k_ref, prob_ref, near_ref, part_ref, dq_ref, acc_ref, q_ref, w_ref):
    groups, rows, heads = shape
    depth = k_ref.shape[1]
    span = 512
    unpack(got_ref, q_ref, w_ref)
    q = q_ref[...]
    for start in range(0, k_ref.shape[0], span):
        k = k_ref[start : start + span]
        edge = edges(shape, q, k, prob_ref, near_ref, part_ref, start)
        step = jnp.dot(edge, k, preferred_element_type=f32)
        if start == 0:
            acc_ref[...] = step
        else:
            acc_ref[...] += step
    acc = acc_ref[...]
    group_rows = rows * heads
    scale = (INDEX_HEADS * depth) ** (-0.5)
    dq = (acc * w_ref[...]).astype(bf16)
    own = acc * q.astype(f32)
    line = lax.broadcasted_iota(jnp.int32, (16, group_rows), 0)
    for g in range(groups):
        piece = slice(g * group_rows, (g + 1) * group_rows)
        dq_ref[g, :group_rows] = dq[piece]
        dw = jnp.sum(own[piece].T, axis=0, keepdims=True) * scale
        high = dw.astype(bf16).astype(f32)
        mid = (dw - high).astype(bf16).astype(f32)
        low = dw - high - mid
        dq_ref[g, group_rows:] = jnp.where(
            line == 0, high, jnp.where(line == 1, mid, jnp.where(line == 2, low, 0.0))
        ).astype(bf16)


def key_backward(slots, got, keys, prob, parts, shape, unit):
    groups, rows, heads = shape
    key_count, depth = keys.shape
    count = groups * rows * heads
    return pl.pallas_call(
        functools.partial(key_kernel, shape, unit),
        in_specs=[SCALARS] + [HELD] * 5,
        out_specs=HELD,
        out_shape=jax.ShapeDtypeStruct((key_count // unit, unit, depth), f32),
        scratch_shapes=[pltpu.VMEM((count, depth), bf16), pltpu.VMEM((count, depth), f32)],
        compiler_params=pltpu.CompilerParams(vmem_limit_bytes=20 << 20),
        name="key_backward",
    )(slots, got, keys, prob, *parts)


def query_backward(got, keys, prob, parts, shape):
    groups, rows, heads = shape
    depth = keys.shape[1]
    count = groups * rows * heads
    return pl.pallas_call(
        functools.partial(query_kernel, shape),
        in_specs=[HELD] * 5,
        out_specs=HELD,
        out_shape=jax.ShapeDtypeStruct((groups, rows * heads + 16, depth), bf16),
        scratch_shapes=[
            pltpu.VMEM((count, depth), f32),
            pltpu.VMEM((count, depth), bf16),
            pltpu.VMEM((count, depth), f32),
        ],
        compiler_params=pltpu.CompilerParams(vmem_limit_bytes=20 << 20),
        name="query_backward",
    )(got, keys, prob, *parts)


def take(a, axis, shift):
    n = lax.axis_size(axis)
    return lax.ppermute(a, axis, [((i + shift) % n, i) for i in range(n)])


def take_z(a, shift):
    place = lambda i: i % 4 * 2 + i % 8 // 4
    return lax.ppermute(a, ("z", "w"), [(place(i + shift), place(i)) for i in range(8)])


def gather_keys(shard, sent):
    found = (take_z(shard, 1), take_z(shard, -1), take_z(shard, 2), sent)
    z1, z3, z2, sent = lax.optimization_barrier(found)
    row = jnp.concatenate([shard, z1, z2, z3], axis=0)
    row, sent = lax.optimization_barrier((row, sent))
    y1, y3, y2 = take(row, "y", 1), take(row, "y", -1), take(row, "y", 2)
    got = lax.all_to_all(sent, HEAD, split_axis=0, concat_axis=0, tiled=True)
    blocks = [row, y1, y3, y2]
    blocks += [take(block, "c", 1) for block in blocks]
    blocks[-1], got = lax.optimization_barrier((blocks[-1], got))
    return blocks, [(dy, dz) for dy in (0, 1, 3, 2) for dz in range(4)], got


def add_up(own, moved):
    moved = lax.optimization_barrier(moved)
    return own.astype(f32) + moved[0].astype(f32) + moved[1].astype(f32) + moved[2].astype(f32)


def pair_sum(kg, unit):
    own = kg.shape[0] // 2
    kg = kg[:own] + take(kg[own:], "c", 1)
    return kg.astype(bf16).reshape(4, 4, unit, kg.shape[-1])


def ring_sum(kg):
    kg = add_up(kg[0], (take(kg[1], "y", -1), take(kg[3], "y", 1), take(kg[2], "y", 2)))
    kg = kg.astype(bf16)
    return add_up(kg[0], (take_z(kg[1], -1), take_z(kg[3], 1), take_z(kg[2], 2)))


def body(latent_queries, latent_keys, index_queries, index_keys, head_weights, visible):
    row_count = latent_queries.shape[0]
    unit = latent_keys.shape[0]
    depth = index_keys.shape[1]
    index_heads = index_queries.shape[1]
    groups = lax.axis_size(HEAD)
    rows = row_count // groups
    me = lax.axis_index(HEAD)
    core = lax.axis_index("c")

    count = rows * index_heads
    sent = pack_index(index_queries.reshape(groups, count, depth), head_weights.reshape(groups, count))
    fill = jnp.zeros((unit, -(depth + latent_keys.shape[1]) % 128), bf16)
    blocks, places, got = gather_keys(jnp.concatenate([index_keys, latent_keys, fill], axis=1), sent)
    chips = len(places)
    key_count = 2 * chips * unit
    dy, dz = (jnp.array([p[i] for p in places], jnp.int32) for i in range(2))
    chip = (lax.axis_index("y") + dy) % 4 * 4 + (lax.axis_index("z") + dz) % 4
    slots = jnp.concatenate([dy * 4 + dz, chips + dy * 4 + dz])
    base = jnp.concatenate([chip * 2 + core, chip * 2 + 1 - core]) * unit
    key_ids = (base[:, None] + jnp.arange(unit, dtype=jnp.int32)[None]).reshape(1, key_count)
    my_visible = lax.dynamic_slice_in_dim(visible, me * rows, rows, 0).reshape(rows, 1)
    shape = (groups, rows, index_heads)

    x, w = lax.axis_index("x"), lax.axis_index("w")
    places = [((x + i) % 4 * 2 + (w + j) % 2) * rows for i in range(4) for j in range(2)]
    *part, keys = head_target(latent_queries, blocks, visible, base, jnp.stack(places), depth)
    moved = (take(part[1], "x", -1), take(part[3], "x", 1), take(part[2], "x", 2))
    near = add_up(part[0], moved)
    parts = (near[0], take(near[1].astype(bf16), "w", 1))
    prob = index_prob(got, keys, my_visible, key_ids, shape)
    kg = pair_sum(key_backward(slots, got, keys, prob, parts, shape, unit), unit)
    kg, prob = lax.optimization_barrier((kg, prob))
    dq = query_backward(got, keys, prob, parts, shape)
    kg = ring_sum(kg)
    kg = jnp.broadcast_to(kg.astype(bf16)[None], (groups, unit, depth))
    back = jnp.concatenate([dq, kg], axis=1)
    back = lax.all_to_all(back, HEAD, split_axis=0, concat_axis=0, tiled=True)
    query_grad = back[:, :count].reshape(row_count, index_heads, depth)
    weight_grad = jnp.sum(back[:, count : count + 16].astype(f32), axis=1)
    key_grad = jnp.sum(back[:, count + 16 :].astype(f32), axis=0)
    return query_grad, weight_grad.reshape(row_count, index_heads), key_grad


def solution(mesh):
    fine = Mesh(mesh.devices.reshape(4, 4, 2, 4, 2), ("y", "z", "c", "x", "w"))
    placed = (
        P(SEQ, HEAD, None),
        P(SEQ, None),
        P(SEQ, HEAD, None),
        P(SEQ, None),
        P(SEQ, HEAD),
        P(SEQ),
    )
    return jax.shard_map(
        body,
        mesh=fine,
        in_specs=placed,
        out_specs=(P(SEQ, HEAD, None), P(SEQ, HEAD), P(SEQ, None)),
        check_vma=False,
    )
```

```python
import functools

import jax
import jax.numpy as jnp
from jax import lax
from jax.experimental import pallas as pl
from jax.experimental.pallas import tpu as pltpu
from jax.sharding import Mesh, PartitionSpec as P

MLA_HEADS = 128
INDEX_HEADS = 64
LOG2E = 1.4426950408889634
mla_scale = 192.0 ** (-0.5)
loss_weight = 16.0
neg_fill = -1e30

SEQ = ("y", "z", "c")
HEAD = ("x", "w")
f32 = jnp.float32
bf16 = jnp.bfloat16
HELD = pl.BlockSpec(memory_space=pltpu.VMEM)
SCALARS = pl.BlockSpec(memory_space=pltpu.SMEM)


def target_kernel(skip, base_ref, offset_ref, q_ref, vis_ref, *refs):
    index_ref, bias_ref, s_ref, p_ref, sum_ref, turn_ref = refs[-6:]
    blocks, outs = refs[:-10], refs[-10:-6]
    heads, depth, rows = q_ref.shape
    key_count = bias_ref.shape[0]
    unit = key_count // base_ref.shape[0]
    span = key_count // len(blocks)
    pairs = heads // 2
    factor = mla_scale * LOG2E

    seen = vis_ref[...]
    for i in range(key_count // unit):
        ids = lax.broadcasted_iota(jnp.int32, (unit, rows), 0) + base_ref[i]
        bias_ref[i * unit : (i + 1) * unit] = jnp.where(ids < seen, 0.0, neg_fill)

    tops, shares = {}, {}
    for step in range(pairs + 2):
        top, total = None, None
        for start in range(0, key_count, span):
            part = slice(start, start + span)
            if step < pairs:
                block = blocks[start // span]
                if step == 0:
                    index_ref[part] = block[:, :skip]
                q = jnp.concatenate([q_ref[2 * step], q_ref[2 * step + 1]], axis=1)
                bias = bias_ref[part]
                s = jnp.dot(block[:, skip : skip + depth], q, preferred_element_type=f32)
                s = s + jnp.concatenate([bias, bias], axis=1)
                s_ref[step % 2, part] = s
                high = jnp.max(s, axis=0, keepdims=True)
                top = high if top is None else jnp.maximum(top, high)
            if 0 <= step - 1 < pairs:
                p = jnp.exp2(s_ref[(step - 1) % 2, part] * factor - tops[step - 1])
                p_ref[(step - 1) % 2, part] = p
                add = jnp.sum(p, axis=0, keepdims=True)
                total = add if total is None else total + add
            if 0 <= step - 2:
                p = p_ref[step % 2, part] * shares[step - 2]
                p = p[:, :rows] + p[:, rows:]
                if step == 2:
                    sum_ref[part] = p
                else:
                    sum_ref[part] += p
        if top is not None:
            tops[step] = top * factor
        if total is not None:
            shares[step - 1] = 1.0 / (total * MLA_HEADS)
    for start in range(0, key_count, rows):
        turn_ref[:, start : start + rows] = sum_ref[start : start + rows].T.astype(bf16)
    for i, out in enumerate(outs):
        for j in range(out.shape[0]):
            start = pl.multiple_of(offset_ref[i * out.shape[0] + j], out.shape[1])
            out[j] = turn_ref[pl.ds(start, out.shape[1])]


def head_target(queries, blocks, visible, base, offsets, skip):
    row_count, heads, depth = queries.shape
    key_count = sum(block.shape[0] for block in blocks)
    turned = queries.transpose(1, 2, 0)
    visible = visible.reshape(1, row_count)
    rows = row_count // offsets.shape[0]
    outs = [jax.ShapeDtypeStruct((offsets.shape[0] // 4, rows, key_count), bf16)] * 4
    return pl.pallas_call(
        functools.partial(target_kernel, skip),
        in_specs=[SCALARS, SCALARS] + [HELD] * (2 + len(blocks)),
        out_specs=[HELD] * 5,
        out_shape=outs + [jax.ShapeDtypeStruct((key_count, skip), bf16)],
        scratch_shapes=[
            pltpu.VMEM((key_count, row_count), f32),
            pltpu.VMEM((2, key_count, 2 * row_count), f32),
            pltpu.VMEM((2, key_count, 2 * row_count), f32),
            pltpu.VMEM((key_count, row_count), f32),
            pltpu.VMEM((row_count, key_count), bf16),
        ],
        compiler_params=pltpu.CompilerParams(vmem_limit_bytes=24 << 20),
        name="head_target",
    )(base, offsets, turned, visible, *blocks)


def pack_kernel(iq_ref, w_ref, out_ref):
    groups, count, depth = iq_ref.shape
    line = lax.broadcasted_iota(jnp.int32, (16, depth), 0)
    for g in range(groups):
        out_ref[g, :count] = iq_ref[g]
        w = w_ref[g : g + 1]
        high = w.astype(bf16).astype(f32)
        mid = (w - high).astype(bf16).astype(f32)
        low = w - high - mid
        lines = jnp.where(line == 0, high, jnp.where(line == 1, mid, jnp.where(line == 2, low, 0.0)))
        out_ref[g, count:] = lines.astype(bf16)


def pack_index(iq, weights):
    groups, count, depth = iq.shape
    return pl.pallas_call(
        pack_kernel,
        in_specs=[HELD] * 2,
        out_specs=HELD,
        out_shape=jax.ShapeDtypeStruct((groups, count + 16, depth), bf16),
        name="pack_index",
    )(iq, weights)


def unpack(got_ref, q_ref, w_ref):
    groups, lines, depth = got_ref.shape
    count = lines - 16
    for g in range(groups):
        piece = slice(g * count, (g + 1) * count)
        q_ref[piece] = got_ref[g, :count]
        w = jnp.sum(got_ref[g, count:].astype(f32), axis=0, keepdims=True)
        w = w * (INDEX_HEADS * depth) ** (-0.5)
        w_ref[piece] = jnp.broadcast_to(w, (depth, count)).T


def prob_kernel(shape, got_ref, k_ref, vis_ref, kid_ref, out_ref, q_ref, w_ref):
    groups, rows, heads = shape
    span = 512
    unpack(got_ref, q_ref, w_ref)
    w = w_ref[:, :1]
    for start in range(0, k_ref.shape[0], span):
        prod = lax.dot_general(
            q_ref[...], k_ref[start : start + span], (((1,), (1,)), ((), ())), preferred_element_type=f32
        )
        part = jnp.maximum(prod, 0.0) * w
        part = part.reshape(groups, rows, heads, span)
        part = jnp.sum(jnp.sum(part, axis=0), axis=1)
        out_ref[:, start : start + span] = part
    logits = jnp.where(kid_ref[...] < vis_ref[...], out_ref[...], neg_fill)
    peak = jnp.max(logits, axis=1, keepdims=True)
    e = jnp.exp2((logits - peak) * LOG2E)
    out_ref[...] = e * (1.0 / jnp.sum(e, axis=1, keepdims=True))


def index_prob(got, keys, visible, key_ids, shape):
    groups, rows, heads = shape
    key_count, depth = keys.shape
    count = groups * rows * heads
    return pl.pallas_call(
        functools.partial(prob_kernel, shape),
        in_specs=[HELD] * 4,
        out_specs=HELD,
        out_shape=jax.ShapeDtypeStruct((rows, key_count), f32),
        scratch_shapes=[pltpu.VMEM((count, depth), bf16), pltpu.VMEM((count, depth), f32)],
        compiler_params=pltpu.CompilerParams(vmem_limit_bytes=20 << 20),
        name="index_prob",
    )(got, keys, visible, key_ids)


def edges(shape, q, k, prob_ref, near_ref, part_ref, start):
    groups, rows, heads = shape
    span = k.shape[0]
    prod = lax.dot_general(q, k, (((1,), (1,)), ((), ())), preferred_element_type=f32)
    here = slice(start, start + span)
    target = near_ref[:, here] + part_ref[:, here].astype(f32)
    grad = loss_weight * (prob_ref[:, start : start + span] - target)
    wide = jnp.broadcast_to(grad[None, :, None, :], (groups, rows, heads, span))
    return jnp.where(prod > 0.0, wide.reshape(q.shape[0], span), 0.0).astype(bf16)


def key_kernel(shape, unit, slot_ref, got_ref, k_ref, prob_ref, near_ref, part_ref, kg_ref, q_ref, w_ref):
    span = 512
    unpack(got_ref, q_ref, w_ref)
    q = q_ref[...]
    lift = (q.astype(f32) * w_ref[...]).T.astype(bf16)
    for start in range(0, k_ref.shape[0], span):
        edge = edges(shape, q, k_ref[start : start + span], prob_ref, near_ref, part_ref, start)
        turned = jnp.dot(lift, edge, preferred_element_type=f32).T
        for i in range(span // unit):
            kg_ref[slot_ref[start // unit + i]] = turned[i * unit : (i + 1) * unit]


def query_kernel(shape, got_ref, k_ref, prob_ref, near_ref, part_ref, dq_ref, acc_ref, q_ref, w_ref):
    groups, rows, heads = shape
    depth = k_ref.shape[1]
    span = 512
    unpack(got_ref, q_ref, w_ref)
    q = q_ref[...]
    for start in range(0, k_ref.shape[0], span):
        k = k_ref[start : start + span]
        edge = edges(shape, q, k, prob_ref, near_ref, part_ref, start)
        step = jnp.dot(edge, k, preferred_element_type=f32)
        if start == 0:
            acc_ref[...] = step
        else:
            acc_ref[...] += step
    acc = acc_ref[...]
    group_rows = rows * heads
    scale = (INDEX_HEADS * depth) ** (-0.5)
    dq = (acc * w_ref[...]).astype(bf16)
    own = acc * q.astype(f32)
    line = lax.broadcasted_iota(jnp.int32, (16, group_rows), 0)
    for g in range(groups):
        piece = slice(g * group_rows, (g + 1) * group_rows)
        dq_ref[g, :group_rows] = dq[piece]
        dw = jnp.sum(own[piece].T, axis=0, keepdims=True) * scale
        high = dw.astype(bf16).astype(f32)
        mid = (dw - high).astype(bf16).astype(f32)
        low = dw - high - mid
        dq_ref[g, group_rows:] = jnp.where(
            line == 0, high, jnp.where(line == 1, mid, jnp.where(line == 2, low, 0.0))
        ).astype(bf16)


def key_backward(slots, got, keys, prob, parts, shape, unit):
    groups, rows, heads = shape
    key_count, depth = keys.shape
    count = groups * rows * heads
    return pl.pallas_call(
        functools.partial(key_kernel, shape, unit),
        in_specs=[SCALARS] + [HELD] * 5,
        out_specs=HELD,
        out_shape=jax.ShapeDtypeStruct((key_count // unit, unit, depth), f32),
        scratch_shapes=[pltpu.VMEM((count, depth), bf16), pltpu.VMEM((count, depth), f32)],
        compiler_params=pltpu.CompilerParams(vmem_limit_bytes=20 << 20),
        name="key_backward",
    )(slots, got, keys, prob, *parts)


def query_backward(got, keys, prob, parts, shape):
    groups, rows, heads = shape
    depth = keys.shape[1]
    count = groups * rows * heads
    return pl.pallas_call(
        functools.partial(query_kernel, shape),
        in_specs=[HELD] * 5,
        out_specs=HELD,
        out_shape=jax.ShapeDtypeStruct((groups, rows * heads + 16, depth), bf16),
        scratch_shapes=[
            pltpu.VMEM((count, depth), f32),
            pltpu.VMEM((count, depth), bf16),
            pltpu.VMEM((count, depth), f32),
        ],
        compiler_params=pltpu.CompilerParams(vmem_limit_bytes=20 << 20),
        name="query_backward",
    )(got, keys, prob, *parts)


def take(a, axis, shift):
    n = lax.axis_size(axis)
    return lax.ppermute(a, axis, [((i + shift) % n, i) for i in range(n)])


def take_z(a, shift):
    place = lambda i: i % 4 * 2 + i % 8 // 4
    return lax.ppermute(a, ("z", "w"), [(place(i + shift), place(i)) for i in range(8)])


def gather_keys(shard, sent):
    found = (take_z(shard, 1), take_z(shard, -1), take_z(shard, 2), sent)
    z1, z3, z2, sent = lax.optimization_barrier(found)
    row = jnp.concatenate([shard, z1, z2, z3], axis=0)
    row, sent = lax.optimization_barrier((row, sent))
    y1, y3, y2 = take(row, "y", 1), take(row, "y", -1), take(row, "y", 2)
    got = lax.all_to_all(sent, HEAD, split_axis=0, concat_axis=0, tiled=True)
    blocks = [row, y1, y3, y2]
    blocks += [take(block, "c", 1) for block in blocks]
    blocks[-1], got = lax.optimization_barrier((blocks[-1], got))
    return blocks, [(dy, dz) for dy in (0, 1, 3, 2) for dz in range(4)], got


def add_up(own, moved):
    moved = lax.optimization_barrier(moved)
    return own.astype(f32) + moved[0].astype(f32) + moved[1].astype(f32) + moved[2].astype(f32)


def pair_sum(kg, unit):
    own = kg.shape[0] // 2
    kg = kg[:own] + take(kg[own:], "c", 1)
    return kg.astype(bf16).reshape(4, 4, unit, kg.shape[-1])


def ring_sum(kg):
    kg = add_up(kg[0], (take(kg[1], "y", -1), take(kg[3], "y", 1), take(kg[2], "y", 2)))
    kg = kg.astype(bf16)
    return add_up(kg[0], (take_z(kg[1], -1), take_z(kg[3], 1), take_z(kg[2], 2)))


def body(latent_queries, latent_keys, index_queries, index_keys, head_weights, visible):
    row_count = latent_queries.shape[0]
    unit = latent_keys.shape[0]
    depth = index_keys.shape[1]
    index_heads = index_queries.shape[1]
    groups = lax.axis_size(HEAD)
    rows = row_count // groups
    me = lax.axis_index(HEAD)
    core = lax.axis_index("c")

    count = rows * index_heads
    sent = pack_index(index_queries.reshape(groups, count, depth), head_weights.reshape(groups, count))
    fill = jnp.zeros((unit, -(depth + latent_keys.shape[1]) % 128), bf16)
    blocks, places, got = gather_keys(jnp.concatenate([index_keys, latent_keys, fill], axis=1), sent)
    chips = len(places)
    key_count = 2 * chips * unit
    dy, dz = (jnp.array([p[i] for p in places], jnp.int32) for i in range(2))
    chip = (lax.axis_index("y") + dy) % 4 * 4 + (lax.axis_index("z") + dz) % 4
    slots = jnp.concatenate([dy * 4 + dz, chips + dy * 4 + dz])
    base = jnp.concatenate([chip * 2 + core, chip * 2 + 1 - core]) * unit
    key_ids = (base[:, None] + jnp.arange(unit, dtype=jnp.int32)[None]).reshape(1, key_count)
    my_visible = lax.dynamic_slice_in_dim(visible, me * rows, rows, 0).reshape(rows, 1)
    shape = (groups, rows, index_heads)

    x, w = lax.axis_index("x"), lax.axis_index("w")
    places = [((x + i) % 4 * 2 + (w + j) % 2) * rows for i in range(4) for j in range(2)]
    *part, keys = head_target(latent_queries, blocks, visible, base, jnp.stack(places), depth)
    moved = (take(part[1], "x", -1), take(part[3], "x", 1), take(part[2], "x", 2))
    near = add_up(part[0], moved)
    parts = (near[0], take(near[1].astype(bf16), "w", 1))
    prob = index_prob(got, keys, my_visible, key_ids, shape)
    kg = pair_sum(key_backward(slots, got, keys, prob, parts, shape, unit), unit)
    kg, prob = lax.optimization_barrier((kg, prob))
    dq = query_backward(got, keys, prob, parts, shape)
    kg = ring_sum(kg)
    kg = jnp.broadcast_to(kg.astype(bf16)[None], (groups, unit, depth))
    back = jnp.concatenate([dq, kg], axis=1)
    back = lax.all_to_all(back, HEAD, split_axis=0, concat_axis=0, tiled=True)
    query_grad = back[:, :count].reshape(row_count, index_heads, depth)
    weight_grad = jnp.sum(back[:, count : count + 16].astype(f32), axis=1)
    key_grad = jnp.sum(back[:, count + 16 :].astype(f32), axis=0)
    return query_grad, weight_grad.reshape(row_count, index_heads), key_grad


def solution(mesh):
    fine = Mesh(mesh.devices.reshape(4, 4, 2, 4, 2), ("y", "z", "c", "x", "w"))
    placed = (
        P(SEQ, HEAD, None),
        P(SEQ, None),
        P(SEQ, HEAD, None),
        P(SEQ, None),
        P(SEQ, HEAD),
        P(SEQ),
    )
    return jax.shard_map(
        body,
        mesh=fine,
        in_specs=placed,
        out_specs=(P(SEQ, HEAD, None), P(SEQ, HEAD), P(SEQ, None)),
        check_vma=False,
    )
```
